256 devices in a mesh: rep: 32 (over x_lo, z, core), tp: 8 (over x_hi, y).
Axes of the slice: x: 4 (x_hi: 2, x_lo: 2; x = x_hi * 2 + x_lo), y: 4, z: 8, core: 2. Of those that a mesh axis runs over, the one named last changes fastest.
Arguments:
- step_index: int32 [1], replicated, may hold values from 0 to 999
- tokens: bfloat16 [32768, 2048], P(('rep', 'tp')), may hold values from -6 to 6
- cotangent: bfloat16 [32768, 2048], P(('rep', 'tp')), may hold values from -6 to 6
- w_query: bfloat16 [32, 2048, 2048], P('rep', None, 'tp'), as said below
- w_key: bfloat16 [32, 2048, 1024], P('rep', None, 'tp'), as said below
- w_value: bfloat16 [32, 2048, 1024], P('rep', None, 'tp'), may hold values from -0.125 to 0.125
- w_out: bfloat16 [32, 2048, 2048], P('rep', 'tp'), may hold values from -0.125 to 0.125
- last_query: bfloat16 [32, 2048, 2048], P('rep', None, 'tp'), may hold values from -0.029907227 to 0.029907227
- last_key: bfloat16 [32, 2048, 1024], P('rep', None, 'tp'), may hold values from -0.029907227 to 0.029907227
- last_value: bfloat16 [32, 2048, 1024], P('rep', None, 'tp'), may hold values from -0.029907227 to 0.029907227
- last_out: bfloat16 [32, 2048, 2048], P('rep', 'tp'), may hold values from -0.029907227 to 0.029907227
- query_gain: float32 [128], replicated, may hold values from 0.5 to 4.5
- key_gain: float32 [128], replicated, may hold values from 0.5 to 4.5
Outputs:
- new_query: bfloat16 [32, 2048, 2048], P('rep', None, 'tp')
- new_key: bfloat16 [32, 2048, 1024], P('rep', None, 'tp')
- new_value: bfloat16 [32, 2048, 1024], P('rep', None, 'tp')
- new_out: bfloat16 [32, 2048, 2048], P('rep', 'tp')
- input_grad: bfloat16 [32768, 2048], P(('rep', 'tp'))
The draws below stay inside these ranges and needn't reach their ends.
Inputs may be any that keep to these rules, and one draw needn't show every extreme that they name: `w_query`: each entry lies within 4 / sqrt(2048) of zero. `w_key`: each entry lies within 4 / sqrt(2048) of zero.
All inputs are finite; a program needn't handle non-finite values.
Results may differ from the reference program's by a relative error of at most 0.024.
The reference program's roundings to bfloat16 on the way count: a program that leaves them out, or rounds other values in their place, can miss the bound.
Values may be sent and summed in bfloat16 or wider, within the bound.
A program may use at most 128 MiB of HBM per device.

```python
import math
import jax
import jax.numpy as jnp
from jax import lax

D = 2048
HEADS = 16
KV = 8
HEAD_DIM = 128
LEN = 1024
REPLICAS = 32
TOKENS = 32768
N_REP = 32
N_TP = 8


def query_base(key):
    return jax.random.truncated_normal(key, -4.0, 4.0, (REPLICAS, D, HEADS * HEAD_DIM), jnp.float32) * D ** (-0.5)


def draw_w_query(key, part):
    return query_base(key).astype(jnp.bfloat16)


def draw_w_key(key, part):
    key = jax.random.fold_in(key, 2)
    fresh = jax.random.truncated_normal(key, -4.0, 4.0, (REPLICAS, D, KV * HEAD_DIM), jnp.float32) * D ** (-0.5)
    return fresh.astype(jnp.bfloat16)


def gain_values(key, lower, upper):
    uniform_part = jax.random.uniform(key, (HEAD_DIM,), jnp.float32)
    return jnp.exp(math.log(lower) + uniform_part * (math.log(upper) - math.log(lower)))


def draw_query_gain(key, part):
    key = jax.random.fold_in(key, 5)
    return gain_values(key, 0.5, 2.0)


def draw_key_gain(key, part):
    key = jax.random.fold_in(key, 6)
    return gain_values(key, 0.5, 2.0)


def level_of(stream_key, extent, split, low, high):
    loudness = 1.0
    for axis_at, blocks in split:
        draws = jax.random.uniform(jax.random.fold_in(jax.random.fold_in(stream_key, 6), axis_at), (blocks,), jnp.float32, low / len(split), high / len(split))
        loudness = loudness * jnp.repeat(jnp.exp(draws), extent[axis_at] // blocks).reshape((-1,) + (1,) * (len(extent) - 1 - axis_at))
    return loudness


def bell_draw(key, dims, spread, most, shards=(), held_as=jnp.bfloat16):
    values = jax.random.normal(key, dims, jnp.float32) * spread
    if len(shards) > 0:
        values = level_of(key, dims, shards, -0.22, 0.18) * values
    return jnp.clip(values, min=-most, max=most).astype(held_as)


def setup_inputs(seed: int = 0) -> dict:
    keys = jax.random.split(jax.random.key(seed), 14)
    return {
        "step_index": jax.random.randint(keys[0], (1,), 0, 1000).astype(jnp.int32),
        "tokens": bell_draw(keys[1], (TOKENS, D), 1.0, 6.0, ((0, 256),)),
        "cotangent": bell_draw(keys[2], (TOKENS, D), 1.0, 6.0, ((0, 256),)),
        "w_query": draw_w_query(jax.random.fold_in(keys[13], 71), 0),
        "w_key": draw_w_key(jax.random.fold_in(keys[13], 71), 0),
        "w_value": bell_draw(keys[5], (REPLICAS, D, KV * HEAD_DIM), D ** -0.5, 0.125, ((0, 32), (2, 8))),
        "w_out": bell_draw(keys[6], (REPLICAS, HEADS * HEAD_DIM, D), (HEADS * HEAD_DIM) ** -0.5, 0.125, ((0, 32), (1, 8))),
        "last_query": bell_draw(keys[7], (REPLICAS, D, HEADS * HEAD_DIM), 0.005, 0.029907227, ((0, 32), (2, 8))),
        "last_key": bell_draw(keys[8], (REPLICAS, D, KV * HEAD_DIM), 0.005, 0.029907227, ((0, 32), (2, 8))),
        "last_value": bell_draw(keys[9], (REPLICAS, D, KV * HEAD_DIM), 0.005, 0.029907227, ((0, 32), (2, 8))),
        "last_out": bell_draw(keys[10], (REPLICAS, HEADS * HEAD_DIM, D), 0.005, 0.029907227, ((0, 32), (1, 8))),
        "query_gain": draw_query_gain(jax.random.fold_in(keys[13], 71), 0),
        "key_gain": draw_key_gain(jax.random.fold_in(keys[13], 71), 0),
    }


EPSILON = 1e-06
MOMENTUM = 0.9
LEARNING_RATE = 0.001
MASKED = -1e+30

def product(pattern, left_in, right_in):
    return jnp.einsum(pattern, left_in.astype(jnp.float32), right_in.astype(jnp.float32))

def rms_rows(values):
    return values * lax.rsqrt(lax.optimization_barrier(jnp.mean(values * values, axis=-1, keepdims=True)) + EPSILON)

def rope_tables(length, head_dim):
    half_dim = head_dim // 2
    inverse = jnp.exp(jnp.arange(half_dim, dtype=jnp.float32) * (-2.0 * math.log(1000000.0) / head_dim))
    angles = jnp.arange(length, dtype=jnp.float32)[:, None] * inverse[None, :]
    return (jnp.cos(angles), jnp.sin(angles))

def shape_heads(raw_rows, gain_vec, cosine_table, sine_table):
    length, total_width = raw_rows.shape
    head_dim = gain_vec.shape[0]
    grouped = raw_rows.reshape(length, total_width // head_dim, head_dim)
    grouped = rms_rows(grouped) * gain_vec.astype(jnp.float32)
    half_dim = head_dim // 2
    first_half = grouped[..., :half_dim]
    second_half = grouped[..., half_dim:]
    cos_part = cosine_table[:, None, :]
    sin_part = sine_table[:, None, :]
    turned = jnp.concatenate([first_half * cos_part - second_half * sin_part, second_half * cos_part + first_half * sin_part], axis=-1)
    return turned.reshape(length, total_width)

def softmax_rows(query_block, key_heads, offset, score_scale):
    block_len = query_block.shape[0]
    length = key_heads.shape[0]
    scores = product('bkgd,tkd->kgbt', query_block, key_heads) * score_scale
    row_pos = offset + jnp.arange(block_len, dtype=jnp.int32)[:, None]
    col_pos = jnp.arange(length, dtype=jnp.int32)[None, :]
    scores = jnp.where(col_pos <= row_pos, scores, MASKED)
    highest = lax.optimization_barrier(jnp.max(scores, axis=-1, keepdims=True))
    raised = jnp.exp(scores - highest)
    return raised / lax.optimization_barrier(jnp.sum(raised, axis=-1, keepdims=True))

def attend(query_rows, key_rows, value_rows, head_dim):
    length = query_rows.shape[0]
    kv_count = key_rows.shape[1] // head_dim
    group_size = query_rows.shape[1] // key_rows.shape[1]
    key_heads = key_rows.reshape(length, kv_count, head_dim)
    value_heads = value_rows.reshape(length, kv_count, head_dim)
    block_len = min(512, length)
    score_scale = head_dim ** (-0.5)
    outputs = []
    for block_at in range(length // block_len):
        offset = block_at * block_len
        query_block = query_rows[offset:offset + block_len].reshape(block_len, kv_count, group_size, head_dim)
        probability = softmax_rows(query_block, key_heads, offset, score_scale)
        combined = product('kgbt,tkd->bkgd', probability.astype(jnp.bfloat16), value_heads)
        outputs.append(combined.reshape(block_len, -1).astype(jnp.bfloat16))
    return jnp.concatenate(outputs, axis=0)

def attend_back(query_rows, key_rows, value_rows, d_attended, head_dim):
    length = query_rows.shape[0]
    kv_count = key_rows.shape[1] // head_dim
    group_size = query_rows.shape[1] // key_rows.shape[1]
    key_heads = key_rows.reshape(length, kv_count, head_dim)
    value_heads = value_rows.reshape(length, kv_count, head_dim)
    block_len = min(512, length)
    score_scale = head_dim ** (-0.5)
    d_keys = jnp.zeros((length, kv_count, head_dim), jnp.float32)
    d_values = jnp.zeros((length, kv_count, head_dim), jnp.float32)
    query_parts = []
    for block_at in range(length // block_len):
        offset = block_at * block_len
        query_block = query_rows[offset:offset + block_len].reshape(block_len, kv_count, group_size, head_dim)
        probability = softmax_rows(query_block, key_heads, offset, score_scale)
        upstream = d_attended[offset:offset + block_len].reshape(block_len, kv_count, group_size, head_dim)
        d_values = d_values + product('kgbt,bkgd->tkd', probability.astype(jnp.bfloat16), upstream)
        d_prob = product('bkgd,tkd->kgbt', upstream, value_heads)
        centred = d_prob - lax.optimization_barrier(jnp.sum(probability * d_prob, axis=-1, keepdims=True))
        d_scores = (probability * centred * score_scale).astype(jnp.bfloat16)
        query_parts.append(product('kgbt,tkd->bkgd', d_scores, key_heads).reshape(block_len, -1))
        d_keys = d_keys + product('kgbt,bkgd->tkd', d_scores, query_block)
    return (jnp.concatenate(query_parts, axis=0), d_keys.reshape(length, -1), d_values.reshape(length, -1))

def advance(weight, last_step, gradient):
    return (weight.astype(jnp.float32) + MOMENTUM * last_step.astype(jnp.float32) - LEARNING_RATE * gradient).astype(jnp.bfloat16)

def average(own_copy, partner):
    return (0.5 * (own_copy.astype(jnp.float32) + partner.astype(jnp.float32))).astype(jnp.bfloat16)

def group_grads(gathered, upstream, joined, out_weight, query_gain, key_gain, cosine_table, sine_table, q_width, k_width):
    head_dim = query_gain.shape[0]
    projected = jnp.dot(gathered, joined, preferred_element_type=jnp.float32)
    q_shaped, q_back = jax.vjp(lambda inner_raw: shape_heads(inner_raw, query_gain, cosine_table, sine_table), projected[:, :q_width])
    k_shaped, k_back = jax.vjp(lambda inner_raw: shape_heads(inner_raw, key_gain, cosine_table, sine_table), projected[:, q_width:q_width + k_width])
    query_rows = q_shaped.astype(jnp.bfloat16)
    key_rows = k_shaped.astype(jnp.bfloat16)
    value_rows = projected[:, q_width + k_width:].astype(jnp.bfloat16)
    attended = attend(query_rows, key_rows, value_rows, head_dim)
    d_attended = lax.dot_general(upstream, out_weight, (((1,), (1,)), ((), ())), preferred_element_type=jnp.float32).astype(jnp.bfloat16)
    grad_out = lax.dot_general(attended, upstream, (((0,), (0,)), ((), ())), preferred_element_type=jnp.float32)
    d_query, d_keys, d_values = attend_back(query_rows, key_rows, value_rows, d_attended, head_dim)
    d_proj = jnp.concatenate([q_back(d_query)[0].astype(jnp.bfloat16), k_back(d_keys)[0].astype(jnp.bfloat16), d_values.astype(jnp.bfloat16)], axis=1)
    grad_joined = lax.dot_general(gathered, d_proj, (((0,), (0,)), ((), ())), preferred_element_type=jnp.float32)
    group_term = lax.dot_general(d_proj, joined, (((1,), (1,)), ((), ())), preferred_element_type=jnp.float32).astype(jnp.bfloat16)
    return (grad_joined, grad_out, group_term)

def reference(step_index, tokens, cotangent, w_query, w_key, w_value, w_out, last_query, last_key, last_value, last_out, query_gain, key_gain):
    q_width = HEADS * HEAD_DIM // N_TP
    k_width = KV * HEAD_DIM // N_TP
    cosine_table, sine_table = rope_tables(LEN, HEAD_DIM)

    def replica_step(replica):
        token_rows = lax.dynamic_slice_in_dim(tokens, replica * LEN, LEN, 0)
        upstream = lax.dynamic_slice_in_dim(cotangent, replica * LEN, LEN, 0)
        normed, norm_back = jax.vjp(rms_rows, token_rows.astype(jnp.float32))
        gathered = normed.astype(jnp.bfloat16)
        query_all = w_query[replica]
        key_all = w_key[replica]
        value_all = w_value[replica]
        out_all = w_out[replica]
        grads_q, grads_k, grads_v, grads_o = ([], [], [], [])
        summed = jnp.zeros((LEN, D), jnp.float32)
        for group_at in range(N_TP):
            joined = jnp.concatenate([query_all[:, group_at * q_width:(group_at + 1) * q_width], key_all[:, group_at * k_width:(group_at + 1) * k_width], value_all[:, group_at * k_width:(group_at + 1) * k_width]], axis=1)
            out_weight = out_all[group_at * q_width:(group_at + 1) * q_width]
            grad_joined, grad_out, group_term = group_grads(gathered, upstream, joined, out_weight, query_gain, key_gain, cosine_table, sine_table, q_width, k_width)
            grads_q.append(grad_joined[:, :q_width])
            grads_k.append(grad_joined[:, q_width:q_width + k_width])
            grads_v.append(grad_joined[:, q_width + k_width:])
            grads_o.append(grad_out)
            summed = summed + group_term.astype(jnp.float32)
        d_tokens = (norm_back(summed)[0] + upstream.astype(jnp.float32)).astype(jnp.bfloat16)
        moved_q = advance(query_all, last_query[replica], jnp.concatenate(grads_q, axis=1))
        moved_k = advance(key_all, last_key[replica], jnp.concatenate(grads_k, axis=1))
        moved_v = advance(value_all, last_value[replica], jnp.concatenate(grads_v, axis=1))
        moved_o = advance(out_all, last_out[replica], jnp.concatenate(grads_o, axis=0))
        return (moved_q, moved_k, moved_v, moved_o, d_tokens)
    moved_q, moved_k, moved_v, moved_o, d_tokens = lax.map(replica_step, jnp.arange(N_REP, dtype=jnp.int32))
    levels = N_REP.bit_length() - 1
    distance = jnp.left_shift(jnp.int32(1), (step_index[0] % levels).astype(jnp.int32))
    new_query = average(moved_q, jnp.roll(moved_q, distance, axis=0))
    new_key = average(moved_k, jnp.roll(moved_k, distance, axis=0))
    new_value = average(moved_v, jnp.roll(moved_v, distance, axis=0))
    new_out = average(moved_o, jnp.roll(moved_o, distance, axis=0))
    return (new_query, new_key, new_value, new_out, d_tokens.reshape(N_REP * LEN, D))
```

```python
import functools
import math

import jax
import jax.numpy as jnp
import numpy as np
from jax import lax
from jax.experimental import pallas as pl
from jax.experimental.pallas import tpu as pltpu
from jax.sharding import PartitionSpec as P

EPSILON = 1e-06
MOMENTUM = 0.9
LEARNING_RATE = 0.001
MASKED = -1e30
MESH = pl.DeviceIdType.MESH
BF16 = jnp.bfloat16
F32 = jnp.float32
HD = 128
SCALE = HD ** (-0.5)
LOG2E = math.log2(math.e)
QB = 256
ROWS, COLS, LEN, QKV, QW = 128, 2048, 1024, 512, 256
X_ROWS = 512

YM, YP, X0, Y2A, Y2B, XM, XP, X2A, X2B = range(9)


def dot(a, b):
    return jnp.dot(a, b, preferred_element_type=F32)


def dot_t(a, b):
    return lax.dot_general(a, b, (((1,), (1,)), ((), ())), preferred_element_type=F32)


def rope_tables(length):
    half = HD // 2
    inverse = np.exp(np.arange(half, dtype=np.float32) * np.float32(-2.0 * math.log(1000000.0) / HD))
    angles = np.arange(length, dtype=np.float32)[:, None] * inverse[None, :].astype(np.float32)
    cosine, sine = np.cos(angles), np.sin(angles)
    return (
        np.concatenate([cosine, cosine], axis=1).astype(np.float32),
        np.concatenate([-sine, sine], axis=1).astype(np.float32),
    )


def kernel(
    shift,
    tokens, cotangent, w_query, w_key, w_value, w_out, l_query, l_key, l_value, l_out,
    query_gain, key_gain, cosine, sine,
    o_query, o_key, o_value, o_out, o_tokens,
    tok, cot_own, normed, cots, normed_t, w_all, l_all, wo, lo, cos_t, sin_t,
    raw, q_rows, k_rows, v_rows, prob, attended, d_att, d_keys, d_values, d_proj,
    arrived, moved, moved_out, partner, partner_out,
    load_sem, store_sem, ag_send, ag_recv, rs_send, rs_recv, ex_send, ex_recv,
):
    reps = lax.axis_size("rep")
    rep = lax.axis_index("rep")
    tp = lax.axis_index("tp")
    h, y = tp // 4, tp % 4
    hx, yp, ym, y2 = 1 - h, (y + 1) % 4, (y + 3) % 4, (y + 2) % 4
    ahead, behind = (rep + shift) % reps, (rep + reps - shift) % reps

    def rows_of(hh, yy):
        return pl.ds(pl.multiple_of((hh * 4 + yy) * ROWS, ROWS), ROWS)

    def half_of(hh, yy, second):
        return pl.ds(pl.multiple_of((hh * 4 + yy) * ROWS + second * (ROWS // 2), ROWS // 2), ROWS // 2)

    own = rows_of(h, y)

    loads = {}

    def load(name, src, dst):
        loads[name] = pltpu.make_async_copy(src, dst, load_sem.at[len(loads)])
        loads[name].start()

    load("tok", tokens, tok)
    load("cot", cotangent, cots.at[own])
    load("cot2", cotangent, cot_own)
    load("wq", w_query, w_all.at[:, 0:256])
    load("wk", w_key, w_all.at[:, 256:384])
    load("wv", w_value, w_all.at[:, 384:512])
    load("cos", cosine, cos_t)
    load("sin", sine, sin_t)
    load("wo", w_out, wo)
    load("lo", l_out, lo)
    load("lq", l_query, l_all.at[:, 0:256])
    load("lk", l_key, l_all.at[:, 256:384])
    load("lv", l_value, l_all.at[:, 384:512])

    barrier = pltpu.get_barrier_semaphore()
    for step in range(1, 8):
        pl.semaphore_signal(barrier, inc=1, device_id={"tp": (tp + step) % 8}, device_id_type=MESH)
    pl.semaphore_signal(barrier, inc=1, device_id={"rep": ahead}, device_id_type=MESH)
    pl.semaphore_signal(barrier, inc=1, device_id={"rep": behind}, device_id_type=MESH)

    loads["tok"].wait()
    x = tok[...].astype(F32)
    normed[own, :] = (x * lax.rsqrt(jnp.mean(x * x, axis=-1, keepdims=True) + EPSILON)).astype(BF16)
    pl.semaphore_wait(barrier, 9)

    copies = {}

    def gather(which, tag, rows, target):
        buf = (normed, cots)[which]
        copies[which, tag] = pltpu.make_async_remote_copy(
            src_ref=buf.at[rows],
            dst_ref=buf.at[rows],
            send_sem=ag_send.at[which, tag],
            recv_sem=ag_recv.at[which, tag],
            device_id={"tp": target},
            device_id_type=MESH,
        )
        copies[which, tag].start()

    def got(which, *tags):
        for tag in tags:
            copies[which, tag].wait_recv()

    t_yp, t_ym, t_x = h * 4 + yp, h * 4 + ym, hx * 4 + y

    def first(which):
        gather(which, YM, own, t_yp)
        gather(which, YP, own, t_ym)
        gather(which, X0, own, t_x)

    def second(which):
        got(which, YM)
        gather(which, Y2A, half_of(h, ym, 0), t_yp)
        got(which, YP)
        gather(which, Y2B, half_of(h, yp, 1), t_ym)
        got(which, X0)
        gather(which, XM, rows_of(hx, y), t_yp)
        gather(which, XP, rows_of(hx, y), t_ym)

    def third(which):
        got(which, Y2A)
        gather(which, X2A, half_of(h, y2, 0), t_x)
        got(which, Y2B)
        gather(which, X2B, half_of(h, y2, 1), t_x)

    def normed_rows(values):
        return values * lax.rsqrt(jnp.mean(values * values, axis=-1, keepdims=True) + EPSILON)

    def turned(values, rows):
        return values * cos_t[rows, :] + pltpu.roll(values, HD // 2, 1) * sin_t[rows, :]

    def project(hh, yy):
        rows = rows_of(hh, yy)
        block = normed[rows, :]
        out = dot(block, w_all[...])
        raw[rows, :] = out[:, :384]
        for head in range(2):
            q_rows[head, rows, :] = turned(
                normed_rows(out[:, head * HD : (head + 1) * HD]) * query_gain[...], rows
            ).astype(BF16)
        k_rows[rows, :] = turned(normed_rows(out[:, 256:384]) * key_gain[...], rows).astype(BF16)
        v_rows[rows, :] = out[:, 384:].astype(BF16)
        normed_t[:, rows] = block.T

    def project_some(pairs):
        for pair in pairs:
            project(*pair)

    def forward(at):
        width = (at + 1) * QB

        def one(head, carry):
            rows = pl.ds(at * QB, QB)
            scores = dot_t(q_rows[head, rows, :], k_rows[0:width, :]) * (SCALE * LOG2E)
            row_pos = at * QB + lax.broadcasted_iota(jnp.int32, (QB, width), 0)
            col_pos = lax.broadcasted_iota(jnp.int32, (QB, width), 1)
            scores = jnp.where(col_pos <= row_pos, scores, MASKED)
            raised = jnp.exp2(scores - jnp.max(scores, axis=-1, keepdims=True))
            p = raised * (1.0 / jnp.sum(raised, axis=-1, keepdims=True))
            prob[head, rows, 0:width] = p
            attended[head, rows, :] = dot(p.astype(BF16), v_rows[0:width, :]).astype(BF16)
            return carry

        lax.fori_loop(0, 2, one, 0)

    def backward(at):
        width = (at + 1) * QB

        for head in range(2):
            rows = pl.ds(at * QB, QB)
            p = prob[head, rows, 0:width]
            up = d_att[head, rows, :]
            d_prob = dot_t(up, v_rows[0:width, :])
            centred = d_prob - jnp.sum(p * d_prob, axis=-1, keepdims=True)
            d_scores = (p * centred * SCALE).astype(BF16)
            d_values[0:width, :] += dot(p.astype(BF16).T, up)
            d_keys[0:width, :] += dot(d_scores.T, q_rows[head, rows, :])
            d_query = dot(d_scores, k_rows[0:width, :])
            d_proj[rows, head * HD : (head + 1) * HD] = unshaped(
                d_query, raw[rows, head * HD : (head + 1) * HD], query_gain, rows
            )

    def unshaped(d_turned, before, gain, rows):
        d_grouped = d_turned * cos_t[rows, :] + pltpu.roll(d_turned * sin_t[rows, :], HD // 2, 1)
        d_norm = d_grouped * gain[...]
        inverse = lax.rsqrt(jnp.mean(before * before, axis=-1, keepdims=True) + EPSILON)
        inner = jnp.mean(before * d_norm, axis=-1, keepdims=True)
        return (inverse * d_norm - before * (inverse * inverse * inverse * inner)).astype(BF16)

    def upstream(hh, yy):
        rows = rows_of(hh, yy)
        out = dot_t(cots[rows, :], wo[...]).astype(BF16)
        d_att[0, rows, :] = out[:, :HD]
        d_att[1, rows, :] = out[:, HD:]

    first(0)
    for name in ("wq", "wk", "wv", "cos", "sin", "cot"):
        loads[name].wait()
    project(h, y)
    second(0)
    project_some([(h, ym), (h, yp), (hx, y)])
    third(0)
    first(1)
    project(h, y2)
    got(0, XM, XP)
    project_some([(hx, ym), (hx, yp)])
    got(0, X2A, X2B)
    project(hx, y2)
    second(1)
    forward(0)
    forward(1)
    third(1)
    loads["wo"].wait()
    loads["lo"].wait()
    forward(2)
    forward(3)
    upstream(h, y)
    upstream(h, ym)
    upstream(h, yp)
    upstream(hx, y)
    upstream(h, y2)
    got(1, XM, XP)
    upstream(hx, ym)
    upstream(hx, yp)
    got(1, X2A, X2B)
    upstream(hx, y2)

    exchange = []

    def send_on(src, dst):
        at = len(exchange)
        copy = pltpu.make_async_remote_copy(
            src_ref=src,
            dst_ref=dst,
            send_sem=ex_send.at[at],
            recv_sem=ex_recv.at[at],
            device_id={"rep": ahead},
            device_id_type=MESH,
        )
        copy.start()
        exchange.append(copy)

    for head in range(2):
        rows = pl.ds(head * HD, HD)
        att_t = attended[head].T

        def out_step(at, carry):
            cols = pl.ds(pl.multiple_of(at * 512, 512), 512)
            grad = dot(att_t, cots[:, cols])
            moved_out[rows, cols] = (
                wo[rows, cols].astype(F32)
                + MOMENTUM * lo[rows, cols].astype(F32)
                - LEARNING_RATE * grad
            ).astype(BF16)
            return carry

        lax.fori_loop(0, 4, out_step, 0)
        send_on(moved_out.at[rows], partner_out.at[rows])

    d_keys[...] = jnp.zeros_like(d_keys)
    d_values[...] = jnp.zeros_like(d_values)
    for at in range(LEN // QB):
        backward(at)

    def key_step(at, carry):
        rows = pl.ds(pl.multiple_of(at * 256, 256), 256)
        d_proj[rows, 256:384] = unshaped(d_keys[rows, :], raw[rows, 256:384], key_gain, rows)
        d_proj[rows, 384:512] = d_values[rows, :].astype(BF16)
        return carry

    lax.fori_loop(0, 4, key_step, 0)

    for copy in copies.values():
        copy.wait_send()

    terms = cots

    def term_step(at, carry):
        rows = pl.ds(pl.multiple_of(at * 256, 256), 256)
        terms[rows, :] = dot_t(d_proj[rows, :], w_all[...]).astype(BF16)
        return carry

    lax.fori_loop(0, 4, term_step, 0)
    scatter = []
    for step in range(1, 8):
        target = (tp + step) % 8
        copy = pltpu.make_async_remote_copy(
            src_ref=terms.at[pl.ds(pl.multiple_of(target * ROWS, ROWS), ROWS)],
            dst_ref=arrived.at[step - 1],
            send_sem=rs_send.at[step - 1],
            recv_sem=rs_recv.at[step - 1],
            device_id={"tp": target},
            device_id_type=MESH,
        )
        copy.start()
        scatter.append(copy)

    for name in ("lq", "lk", "lv"):
        loads[name].wait()
    for at in range(COLS // X_ROWS):

        def weight_step(sub, carry):
            rows = pl.ds(pl.multiple_of(at * X_ROWS + sub * 256, 256), 256)
            grad = dot(normed_t[rows, :], d_proj[...])
            moved[rows, :] = (
                w_all[rows, :].astype(F32)
                + MOMENTUM * l_all[rows, :].astype(F32)
                - LEARNING_RATE * grad
            ).astype(BF16)
            return carry

        lax.fori_loop(0, X_ROWS // 256, weight_step, 0)
        rows = pl.ds(at * X_ROWS, X_ROWS)
        send_on(moved.at[rows], partner.at[rows])

    for copy in scatter:
        copy.wait_recv()
    loads["cot2"].wait()

    def token_step(at, carry):
        rows = pl.ds(pl.multiple_of(at * 32, 32), 32)
        total = terms[pl.ds(pl.multiple_of(tp * ROWS + at * 32, 32), 32), :].astype(F32)
        for step in range(7):
            total = total + arrived[step, rows, :].astype(F32)
        x = tok[rows, :].astype(F32)
        inverse = lax.rsqrt(jnp.mean(x * x, axis=-1, keepdims=True) + EPSILON)
        inner = jnp.mean(x * total, axis=-1, keepdims=True)
        tok[rows, :] = (
            inverse * total
            - x * (inverse * inverse * inverse * inner)
            + cot_own[rows, :].astype(F32)
        ).astype(BF16)
        return carry

    lax.fori_loop(0, ROWS // 32, token_step, 0)
    stores = []

    def store(src, dst):
        copy = pltpu.make_async_copy(src, dst, store_sem.at[len(stores)])
        copy.start()
        stores.append(copy)

    store(tok, o_tokens)

    def averaged(mine, theirs, rows):
        theirs[rows, :] = (0.5 * (mine[rows, :].astype(F32) + theirs[rows, :].astype(F32))).astype(BF16)

    for head in range(2):
        exchange[head].wait_recv()
        rows = pl.ds(head * HD, HD)
        averaged(moved_out, partner_out, rows)
        store(partner_out.at[rows], o_out.at[rows])
    for at in range(COLS // X_ROWS):
        exchange[2 + at].wait_recv()
        rows = pl.ds(at * X_ROWS, X_ROWS)
        averaged(moved, partner, rows)
        store(partner.at[rows, 0:256], o_query.at[rows])
        store(partner.at[rows, 256:384], o_key.at[rows])
        store(partner.at[rows, 384:512], o_value.at[rows])
    for copy in scatter:
        copy.wait_send()
    for copy in exchange:
        copy.wait_send()
    for copy in stores:
        copy.wait()


def training_step(exponent, arrays):
    def vmem(*shape, dtype=BF16):
        return pltpu.VMEM(shape, dtype)

    dma = pltpu.SemaphoreType.DMA
    any_spec = pl.BlockSpec(memory_space=pl.ANY)
    vmem_spec = pl.BlockSpec(memory_space=pltpu.VMEM)
    return pl.pallas_call(
        functools.partial(kernel, 1 << exponent),
        out_shape=(
            jax.ShapeDtypeStruct((COLS, 256), BF16),
            jax.ShapeDtypeStruct((COLS, 128), BF16),
            jax.ShapeDtypeStruct((COLS, 128), BF16),
            jax.ShapeDtypeStruct((256, COLS), BF16),
            jax.ShapeDtypeStruct((ROWS, COLS), BF16),
        ),
        in_specs=[any_spec] * 10 + [vmem_spec] * 2 + [any_spec] * 2,
        out_specs=(any_spec,) * 5,
        scratch_shapes=[
            vmem(ROWS, COLS),
            vmem(ROWS, COLS),
            vmem(LEN, COLS),
            vmem(LEN, COLS),
            vmem(COLS, LEN),
            vmem(COLS, QKV),
            vmem(COLS, QKV),
            vmem(QW, COLS),
            vmem(QW, COLS),
            vmem(LEN, HD, dtype=F32),
            vmem(LEN, HD, dtype=F32),
            vmem(LEN, 384, dtype=F32),
            vmem(2, LEN, HD),
            vmem(LEN, HD),
            vmem(LEN, HD),
            vmem(2, LEN, LEN, dtype=F32),
            vmem(2, LEN, HD),
            vmem(2, LEN, HD),
            vmem(LEN, HD, dtype=F32),
            vmem(LEN, HD, dtype=F32),
            vmem(LEN, QKV),
            vmem(7, ROWS, COLS),
            vmem(COLS, QKV),
            vmem(QW, COLS),
            vmem(COLS, QKV),
            vmem(QW, COLS),
            dma((13,)),
            dma((3 + 3 * (COLS // X_ROWS),)),
            dma((2, 9)),
            dma((2, 9)),
            dma((7,)),
            dma((7,)),
            dma((2 + COLS // X_ROWS,)),
            dma((2 + COLS // X_ROWS,)),
        ],
        compiler_params=pltpu.CompilerParams(
            collective_id=exponent, has_side_effects=True, vmem_limit_bytes=60 << 20
        ),
        cost_estimate=pl.CostEstimate(
            flops=11_000_000_000, bytes_accessed=12_000_000, transcendentals=2_000_000
        ),
    )(*arrays)


def per_device(
    step_index, tokens, cotangent, w_query, w_key, w_value, w_out,
    last_query, last_key, last_value, last_out, query_gain, key_gain,
):
    levels = lax.axis_size("rep").bit_length() - 1
    cosine, sine = rope_tables(LEN)
    arrays = (
        tokens, cotangent, w_query[0], w_key[0], w_value[0], w_out[0],
        last_query[0], last_key[0], last_value[0], last_out[0],
        query_gain[None], key_gain[None], jnp.asarray(cosine), jnp.asarray(sine),
    )
    new_query, new_key, new_value, new_out, d_tokens = lax.switch(
        step_index[0] % levels,
        [functools.partial(training_step, exponent) for exponent in range(levels)],
        arrays,
    )
    return (new_query[None], new_key[None], new_value[None], new_out[None], d_tokens)


def solution(mesh):
    placed = (
        P(),
        P(("rep", "tp"), None),
        P(("rep", "tp"), None),
        P("rep", None, "tp"),
        P("rep", None, "tp"),
        P("rep", None, "tp"),
        P("rep", "tp", None),
        P("rep", None, "tp"),
        P("rep", None, "tp"),
        P("rep", None, "tp"),
        P("rep", "tp", None),
        P(),
        P(),
    )
    return jax.shard_map(
        per_device,
        mesh=mesh,
        in_specs=placed,
        out_specs=(
            P("rep", None, "tp"),
            P("rep", None, "tp"),
            P("rep", None, "tp"),
            P("rep", "tp", None),
            P(("rep", "tp"), None),
        ),
        check_vma=False,
    )
```

```python
import functools
import math

import jax
import jax.numpy as jnp
import numpy as np
from jax import lax
from jax.experimental import pallas as pl
from jax.experimental.pallas import tpu as pltpu
from jax.sharding import PartitionSpec as P

EPSILON = 1e-06
MOMENTUM = 0.9
LEARNING_RATE = 0.001
MASKED = -1e30
MESH = pl.DeviceIdType.MESH
BF16 = jnp.bfloat16
F32 = jnp.float32
HD = 128
SCALE = HD ** (-0.5)
LOG2E = math.log2(math.e)
QB = 256
ROWS, COLS, LEN, QKV, QW = 128, 2048, 1024, 512, 256

YM, YP, X0, Y2A, Y2B, XM, XP, X2A, X2B = range(9)
RC, RP, RM, HA, HB, NX, NMA, NMB, NPA, NPB = range(10)


def dot(a, b):
    return jnp.dot(a, b, preferred_element_type=F32)


def dot_t(a, b):
    return lax.dot_general(a, b, (((1,), (1,)), ((), ())), preferred_element_type=F32)


def rope_tables(length):
    half = HD // 2
    inverse = np.exp(np.arange(half, dtype=np.float32) * np.float32(-2.0 * math.log(1000000.0) / HD))
    angles = np.arange(length, dtype=np.float32)[:, None] * inverse[None, :].astype(np.float32)
    cosine, sine = np.cos(angles), np.sin(angles)
    return (
        np.concatenate([cosine, cosine], axis=1).astype(np.float32),
        np.concatenate([-sine, sine], axis=1).astype(np.float32),
    )


def kernel(
    shift,
    tokens, cotangent, w_query, w_key, w_value, w_out, l_query, l_key, l_value, l_out,
    query_gain, key_gain, cosine, sine,
    o_query, o_key, o_value, o_out, o_tokens,
    tok, cot_own, normed, cots, normed_t, w_all, l_all, wo, lo, cos_t, sin_t,
    raw, q_rows, k_rows, v_rows, prob, att_t, d_att, d_keys, d_values, d_proj,
    arrived, moved, moved_out, partner, partner_out, relay,
    load_sem, store_sem, ag_send, ag_recv, rs_send, rs_recv, ex_send, ex_recv, relay_send, relay_recv,
):
    reps = lax.axis_size("rep")
    rep = lax.axis_index("rep")
    tp = lax.axis_index("tp")
    h, y = tp // 4, tp % 4
    hx, yp, ym, y2 = 1 - h, (y + 1) % 4, (y + 3) % 4, (y + 2) % 4
    ahead, behind = (rep + shift) % reps, (rep + reps - shift) % reps
    relayed = shift == 4
    ring = 16

    def along(start, by):
        return start // ring * ring + (start % ring + ring + by) % ring

    via = along(rep, -6)
    via_ahead = (along(rep, 6) + shift) % reps
    via_behind = along(behind, -6)

    def rows_of(hh, yy):
        return pl.ds(pl.multiple_of((hh * 4 + yy) * ROWS, ROWS), ROWS)

    def half_of(hh, yy, second):
        return pl.ds(pl.multiple_of((hh * 4 + yy) * ROWS + second * (ROWS // 2), ROWS // 2), ROWS // 2)

    own = rows_of(h, y)

    loads = {}

    def load(name, src, dst):
        loads[name] = pltpu.make_async_copy(src, dst, load_sem.at[len(loads)])
        loads[name].start()

    load("tok", tokens, tok)
    load("cot", cotangent, cots.at[own])
    load("cot2", cotangent, cot_own)
    load("wq", w_query, w_all.at[:, 0:256])
    load("wk", w_key, w_all.at[:, 256:384])
    load("wv", w_value, w_all.at[:, 384:512])
    load("cos", cosine, cos_t)
    load("sin", sine, sin_t)
    load("wo", w_out, wo)
    load("lo", l_out, lo)
    load("lq", l_query, l_all.at[:, 0:256])
    load("lk", l_key, l_all.at[:, 256:384])
    load("lv", l_value, l_all.at[:, 384:512])

    barrier = pltpu.get_barrier_semaphore()
    for step in range(1, 8):
        pl.semaphore_signal(barrier, inc=1, device_id={"tp": (tp + step) % 8}, device_id_type=MESH)
    partners = [ahead, behind]
    if relayed:
        partners += [via, along(rep, 6), via_ahead, via_behind]
    for device in partners:
        pl.semaphore_signal(barrier, inc=1, device_id={"rep": device}, device_id_type=MESH)

    loads["tok"].wait()
    x = tok[...].astype(F32)
    normed[own, :] = (x * lax.rsqrt(jnp.mean(x * x, axis=-1, keepdims=True) + EPSILON)).astype(BF16)
    pl.semaphore_wait(barrier, 7 + len(partners))

    t_yp, t_ym, t_x = h * 4 + yp, h * 4 + ym, hx * 4 + y
    own_half = (half_of(h, ym, 0), half_of(h, yp, 1))
    far_half = (half_of(h, y2, 0), half_of(h, y2, 1))
    plans = {
        YM: (own, t_yp),
        YP: (own, t_ym),
        X0: (own, t_x),
        Y2A: (own_half[0], t_yp),
        Y2B: (own_half[1], t_ym),
        XM: (rows_of(hx, y), t_yp),
        XP: (rows_of(hx, y), t_ym),
        X2A: (far_half[0], t_x),
        X2B: (far_half[1], t_x),
    }

    def gather(which, tag):
        rows, target = plans[tag]
        buf = (normed, cots)[which]
        return pltpu.make_async_remote_copy(
            src_ref=buf.at[rows],
            dst_ref=buf.at[rows],
            send_sem=ag_send.at[which, tag],
            recv_sem=ag_recv.at[which, tag],
            device_id={"tp": target},
            device_id_type=MESH,
        )

    def start(which, *tags):
        for tag in tags:
            gather(which, tag).start()

    def got(which, *tags):
        for tag in tags:
            gather(which, tag).wait_recv()

    def first(which):
        start(which, YM, YP, X0)

    def second(which):
        got(which, YM)
        start(which, Y2A)
        got(which, YP)
        start(which, Y2B)
        got(which, X0)
        start(which, XM, XP)

    def third(which):
        got(which, Y2A)
        start(which, X2A)
        got(which, Y2B)
        start(which, X2B)

    order = tuple(zip((0, 0, 0, 1, 0, 1, 1, 1), (0, 3, 1, 0, 2, 3, 1, 2)))

    def over_blocks(offsets, before, work, after=None):
        def body(i, carry):
            far, turn = carry
            for step, action in before.items():
                pl.when(i == step)(action)
            hh = (h + far % 2) % 2
            work(rows_of(hh, (y + turn % 4) % 4))
            for step, action in (after or {}).items():
                pl.when(i == step)(action)
            return far // 2, turn // 4

        far = sum(bit << i for i, (bit, _) in enumerate(offsets))
        turn = sum(step << (2 * i) for i, (_, step) in enumerate(offsets))
        lax.fori_loop(0, 8, body, (jnp.int32(far), jnp.int32(turn)))

    def normed_rows(values):
        return values * lax.rsqrt(jnp.mean(values * values, axis=-1, keepdims=True) + EPSILON)

    def turned(values, rows):
        return values * cos_t[rows, :] + pltpu.roll(values, HD // 2, 1) * sin_t[rows, :]

    def project(rows):
        block = normed[rows, :]
        out = dot(block, w_all[...])
        raw[rows, :] = out[:, :384]
        for head in range(2):
            q_rows[head, rows, :] = turned(
                normed_rows(out[:, head * HD : (head + 1) * HD]) * query_gain[...], rows
            ).astype(BF16)
        k_rows[rows, :] = turned(normed_rows(out[:, 256:384]) * key_gain[...], rows).astype(BF16)
        v_rows[rows, :] = out[:, 384:].astype(BF16)
        normed_t[:, rows] = block.T

    def blocks_of_queries(start_at, width, work):
        def body(i, carry):
            head, at = i % 2, start_at + i // 2
            first_row = pl.multiple_of(at * QB, QB)
            work(head, first_row, pl.ds(first_row, QB), width)
            return carry

        lax.fori_loop(0, 4, body, 0)

    def forward(head, first_row, rows, width):
        scores = dot_t(q_rows[head, rows, :], k_rows[0:width, :]) * (SCALE * LOG2E)
        row_pos = first_row + lax.broadcasted_iota(jnp.int32, (QB, width), 0)
        col_pos = lax.broadcasted_iota(jnp.int32, (QB, width), 1)
        scores = jnp.where(col_pos <= row_pos, scores, MASKED)
        raised = jnp.exp2(scores - jnp.max(scores, axis=-1, keepdims=True))
        p = raised * (1.0 / jnp.sum(raised, axis=-1, keepdims=True))
        prob[head, rows, 0:width] = p
        out = dot(p.astype(BF16), v_rows[0:width, :]).astype(BF16)
        att_t[pl.ds(pl.multiple_of(head * HD, HD), HD), rows] = out.T

    def backward(head, first_row, rows, width):
        p = prob[head, rows, 0:width]
        up = d_att[head, rows, :]
        d_prob = dot_t(up, v_rows[0:width, :])
        centred = d_prob - jnp.sum(p * d_prob, axis=-1, keepdims=True)
        d_scores = (p * centred * SCALE).astype(BF16)
        d_values[0:width, :] += dot(p.astype(BF16).T, up)
        d_keys[0:width, :] += dot(d_scores.T, q_rows[head, rows, :])
        d_query = dot(d_scores, k_rows[0:width, :])
        cols = pl.ds(pl.multiple_of(head * HD, HD), HD)
        d_proj[rows, cols] = unshaped(d_query, raw[rows, cols], query_gain, rows)

    def unshaped(d_turned, before, gain, rows):
        d_grouped = d_turned * cos_t[rows, :] + pltpu.roll(d_turned * sin_t[rows, :], HD // 2, 1)
        d_norm = d_grouped * gain[...]
        inverse = lax.rsqrt(jnp.mean(before * before, axis=-1, keepdims=True) + EPSILON)
        inner = jnp.mean(before * d_norm, axis=-1, keepdims=True)
        return (inverse * d_norm - before * (inverse * inverse * inverse * inner)).astype(BF16)

    def upstream(rows):
        out = dot_t(cots[rows, :], wo[...]).astype(BF16)
        d_att[0, rows, :] = out[:, :HD]
        d_att[1, rows, :] = out[:, HD:]

    def pass_on_first():
        third(0)
        first(1)

    first(0)
    for name in ("wq", "wk", "wv", "cos", "sin", "cot"):
        loads[name].wait()
    over_blocks(
        order,
        {
            1: lambda: second(0),
            4: pass_on_first,
            5: lambda: got(0, XM, XP),
            7: lambda: got(0, X2A, X2B),
        },
        project,
    )
    second(1)
    blocks_of_queries(0, LEN // 2, forward)
    third(1)
    blocks_of_queries(2, LEN, forward)
    loads["wo"].wait()
    loads["lo"].wait()
    over_blocks(order, {5: lambda: got(1, XM, XP), 7: lambda: got(1, X2A, X2B)}, upstream)

    def exchanged(at, mine, theirs):
        return pltpu.make_async_remote_copy(
            src_ref=mine,
            dst_ref=theirs,
            send_sem=ex_send.at[at],
            recv_sem=ex_recv.at[at],
            device_id={"rep": ahead},
            device_id_type=MESH,
        )

    def exchanged_out(at):
        cols = pl.ds(pl.multiple_of(at * 512, 512), 512)
        return exchanged(at, moved_out.at[:, cols], partner_out.at[:, cols])

    def exchanged_in(at):
        rows = pl.ds(pl.multiple_of(at * 256, 256), 256)
        return exchanged(4 + at, moved.at[rows], partner.at[rows])

    def relay_first(at, mine):
        return pltpu.make_async_remote_copy(
            src_ref=mine,
            dst_ref=relay.at[at],
            send_sem=ex_send.at[4 * at + 3],
            recv_sem=relay_recv.at[at],
            device_id={"rep": via},
            device_id_type=MESH,
        )

    def relay_leg(at):
        return pltpu.make_async_remote_copy(
            src_ref=relay.at[at],
            dst_ref=partner_out.at[:, 1536:2048] if at == 0 else partner.at[1024 * at - 256 : 1024 * at],
            send_sem=relay_send.at[at],
            recv_sem=ex_recv.at[4 * at + 3],
            device_id={"rep": via_ahead},
            device_id_type=MESH,
        )

    def relay_on(at):
        if relayed:
            relay_first(at, relay.at[at]).wait_recv()
            relay_leg(at).start()

    def send_chunk(at, group, direct, mine):
        if relayed:
            pl.when(at % 4 != 3)(lambda: direct.start())
            pl.when(at % 4 == 3)(lambda: relay_first(group, mine).start())
        else:
            direct.start()

    def out_step(at, carry):
        cols = pl.ds(pl.multiple_of(at * 512, 512), 512)
        grad = dot(att_t[...], cots[:, cols])
        moved_out[:, cols] = (
            wo[:, cols].astype(F32)
            + MOMENTUM * lo[:, cols].astype(F32)
            - LEARNING_RATE * grad
        ).astype(BF16)
        send_chunk(at, 0, exchanged_out(at), moved_out.at[:, cols])
        return carry

    lax.fori_loop(0, 4, out_step, 0)
    d_keys[...] = jnp.zeros_like(d_keys)
    d_values[...] = jnp.zeros_like(d_values)
    blocks_of_queries(0, LEN // 2, backward)
    blocks_of_queries(2, LEN, backward)

    def key_step(at, carry):
        rows = pl.ds(pl.multiple_of(at * 256, 256), 256)
        d_proj[rows, 256:384] = unshaped(d_keys[rows, :], raw[rows, 256:384], key_gain, rows)
        d_proj[rows, 384:512] = d_values[rows, :].astype(BF16)
        return carry

    lax.fori_loop(0, 4, key_step, 0)

    relay_on(0)
    for which in range(2):
        for tag in plans:
            gather(which, tag).wait_send()

    terms = cots
    first_half, second_half = pl.ds(0, ROWS // 2), pl.ds(ROWS // 2, ROWS // 2)
    routes = {
        RC: (rows_of(hx, y2), arrived.at[0], t_x),
        RP: (rows_of(hx, yp), arrived.at[1], t_yp),
        RM: (rows_of(hx, ym), arrived.at[2], t_ym),
        HA: (half_of(h, y2, 0), arrived.at[3, first_half], t_ym),
        HB: (half_of(h, y2, 1), arrived.at[3, second_half], t_yp),
        NX: (rows_of(hx, y), arrived.at[6], t_x),
        NMA: (half_of(h, ym, 0), arrived.at[4, first_half], t_ym),
        NMB: (half_of(h, ym, 1), arrived.at[4, second_half], t_ym),
        NPA: (half_of(h, yp, 0), arrived.at[5, first_half], t_yp),
        NPB: (half_of(h, yp, 1), arrived.at[5, second_half], t_yp),
    }

    def scatter(tag):
        rows, dst, target = routes[tag]
        return pltpu.make_async_remote_copy(
            src_ref=terms.at[rows],
            dst_ref=dst,
            send_sem=rs_send.at[tag],
            recv_sem=rs_recv.at[tag],
            device_id={"tp": target},
            device_id_type=MESH,
        )

    def add(tag, *arrivals):
        rows = routes[tag][0]
        total = terms[rows, :].astype(F32)
        for arrival in arrivals:
            total = total + arrival.astype(F32)
        terms[rows, :] = total.astype(BF16)
        scatter(tag).start()

    def term(rows):
        terms[rows, :] = dot_t(d_proj[rows, :], w_all[...]).astype(BF16)

    over_blocks(
        order[::-1],
        {},
        term,
        {
            0: lambda: scatter(RC).start(),
            1: lambda: scatter(RP).start(),
            2: lambda: scatter(RM).start(),
            5: lambda: scatter(NPA).start(),
            6: lambda: scatter(NMB).start(),
        },
    )

    for name in ("lq", "lk", "lv"):
        loads[name].wait()

    def weight_step(at, carry):
        rows = pl.ds(pl.multiple_of(at * 256, 256), 256)
        grad = dot(normed_t[rows, :], d_proj[...])
        moved[rows, :] = (
            w_all[rows, :].astype(F32)
            + MOMENTUM * l_all[rows, :].astype(F32)
            - LEARNING_RATE * grad
        ).astype(BF16)
        send_chunk(at, 1 + at // 4, exchanged_in(at), moved.at[rows])
        return carry

    lax.fori_loop(0, 8, weight_step, 0)

    scatter(RC).wait_recv()
    add(HA, arrived[0, first_half, :])
    add(HB, arrived[0, second_half, :])
    scatter(RP).wait_recv()
    scatter(RM).wait_recv()
    add(NX, arrived[1], arrived[2])
    scatter(HA).wait_recv()
    add(NMA, arrived[3, first_half, :])
    scatter(HB).wait_recv()
    add(NPB, arrived[3, second_half, :])
    relay_on(1)
    for tag in (NMA, NMB, NPA, NPB, NX):
        scatter(tag).wait_recv()
    loads["cot2"].wait()

    def token_step(at, carry):
        rows = pl.ds(pl.multiple_of(at * 32, 32), 32)
        total = terms[pl.ds(pl.multiple_of(tp * ROWS + at * 32, 32), 32), :].astype(F32)
        for slot in range(4, 7):
            total = total + arrived[slot, rows, :].astype(F32)
        x = tok[rows, :].astype(F32)
        inverse = lax.rsqrt(jnp.mean(x * x, axis=-1, keepdims=True) + EPSILON)
        inner = jnp.mean(x * total, axis=-1, keepdims=True)
        tok[rows, :] = (
            inverse * total
            - x * (inverse * inverse * inverse * inner)
            + cot_own[rows, :].astype(F32)
        ).astype(BF16)
        return carry

    lax.fori_loop(0, ROWS // 32, token_step, 0)
    store_tokens = pltpu.make_async_copy(tok, o_tokens, store_sem.at[28])
    store_tokens.start()
    relay_on(2)

    def averaged(mine, theirs):
        return (0.5 * (mine.astype(F32) + theirs.astype(F32))).astype(BF16)

    def stored_out(at):
        cols = pl.ds(pl.multiple_of(at * 512, 512), 512)
        return (pltpu.make_async_copy(partner_out.at[:, cols], o_out.at[:, cols], store_sem.at[at]),)

    def stored_in(at):
        rows = pl.ds(pl.multiple_of(at * 256, 256), 256)
        return tuple(
            pltpu.make_async_copy(partner.at[rows, cols], out.at[rows], store_sem.at[4 + 3 * at + i])
            for i, (cols, out) in enumerate(
                ((pl.ds(0, 256), o_query), (pl.ds(256, 128), o_key), (pl.ds(384, 128), o_value))
            )
        )

    def average_out(at, carry):
        exchanged_out(at).wait_recv()
        cols = pl.ds(pl.multiple_of(at * 512, 512), 512)
        partner_out[:, cols] = averaged(moved_out[:, cols], partner_out[:, cols])
        for copy in stored_out(at):
            copy.start()
        return carry

    def average_in(at, carry):
        exchanged_in(at).wait_recv()
        rows = pl.ds(pl.multiple_of(at * 256, 256), 256)
        partner[rows, :] = averaged(moved[rows, :], partner[rows, :])
        for copy in stored_in(at):
            copy.start()
        return carry

    def finish_out(at, carry):
        exchanged_out(at).wait_send()
        for copy in stored_out(at):
            copy.wait()
        return carry

    def finish_in(at, carry):
        exchanged_in(at).wait_send()
        for copy in stored_in(at):
            copy.wait()
        return carry

    lax.fori_loop(0, 4, average_out, 0)
    lax.fori_loop(0, 8, average_in, 0)
    lax.fori_loop(0, 4, finish_out, 0)
    lax.fori_loop(0, 8, finish_in, 0)
    for tag in routes:
        scatter(tag).wait_send()
    if relayed:
        for at in range(3):
            relay_leg(at).wait_send()
    store_tokens.wait()


def training_step(exponent, arrays):
    def vmem(*shape, dtype=BF16):
        return pltpu.VMEM(shape, dtype)

    dma = pltpu.SemaphoreType.DMA
    any_spec = pl.BlockSpec(memory_space=pl.ANY)
    vmem_spec = pl.BlockSpec(memory_space=pltpu.VMEM)
    return pl.pallas_call(
        functools.partial(kernel, 1 << exponent),
        out_shape=(
            jax.ShapeDtypeStruct((COLS, 256), BF16),
            jax.ShapeDtypeStruct((COLS, 128), BF16),
            jax.ShapeDtypeStruct((COLS, 128), BF16),
            jax.ShapeDtypeStruct((256, COLS), BF16),
            jax.ShapeDtypeStruct((ROWS, COLS), BF16),
        ),
        in_specs=[any_spec] * 10 + [vmem_spec] * 2 + [any_spec] * 2,
        out_specs=(any_spec,) * 5,
        scratch_shapes=[
            vmem(ROWS, COLS),
            vmem(ROWS, COLS),
            vmem(LEN, COLS),
            vmem(LEN, COLS),
            vmem(COLS, LEN),
            vmem(COLS, QKV),
            vmem(COLS, QKV),
            vmem(QW, COLS),
            vmem(QW, COLS),
            vmem(LEN, HD, dtype=F32),
            vmem(LEN, HD, dtype=F32),
            vmem(LEN, 384, dtype=F32),
            vmem(2, LEN, HD),
            vmem(LEN, HD),
            vmem(LEN, HD),
            vmem(2, LEN, LEN, dtype=F32),
            vmem(QW, LEN),
            vmem(2, LEN, HD),
            vmem(LEN, HD, dtype=F32),
            vmem(LEN, HD, dtype=F32),
            vmem(LEN, QKV),
            vmem(7, ROWS, COLS),
            vmem(COLS, QKV),
            vmem(QW, COLS),
            vmem(COLS, QKV),
            vmem(QW, COLS),
            vmem(3, 256, 512),
            dma((13,)),
            dma((29,)),
            dma((2, 9)),
            dma((2, 9)),
            dma((10,)),
            dma((10,)),
            dma((12,)),
            dma((12,)),
            dma((3,)),
            dma((3,)),
        ],
        compiler_params=pltpu.CompilerParams(
            collective_id=exponent, has_side_effects=True, vmem_limit_bytes=60 << 20
        ),
        cost_estimate=pl.CostEstimate(
            flops=11_000_000_000, bytes_accessed=12_000_000, transcendentals=2_000_000
        ),
    )(*arrays)


def per_device(
    step_index, tokens, cotangent, w_query, w_key, w_value, w_out,
    last_query, last_key, last_value, last_out, query_gain, key_gain,
):
    levels = lax.axis_size("rep").bit_length() - 1
    cosine, sine = rope_tables(LEN)
    arrays = (
        tokens, cotangent, w_query[0], w_key[0], w_value[0], w_out[0],
        last_query[0], last_key[0], last_value[0], last_out[0],
        query_gain[None], key_gain[None], jnp.asarray(cosine), jnp.asarray(sine),
    )
    new_query, new_key, new_value, new_out, d_tokens = lax.switch(
        step_index[0] % levels,
        [functools.partial(training_step, exponent) for exponent in range(levels)],
        arrays,
    )
    return (new_query[None], new_key[None], new_value[None], new_out[None], d_tokens)


def solution(mesh):
    placed = (
        P(),
        P(("rep", "tp"), None),
        P(("rep", "tp"), None),
        P("rep", None, "tp"),
        P("rep", None, "tp"),
        P("rep", None, "tp"),
        P("rep", "tp", None),
        P("rep", None, "tp"),
        P("rep", None, "tp"),
        P("rep", None, "tp"),
        P("rep", "tp", None),
        P(),
        P(),
    )
    return jax.shard_map(
        per_device,
        mesh=mesh,
        in_specs=placed,
        out_specs=(
            P("rep", None, "tp"),
            P("rep", None, "tp"),
            P("rep", None, "tp"),
            P("rep", "tp", None),
            P(("rep", "tp"), None),
        ),
        check_vma=False,
    )
```

```python
import functools
import math

import jax
import jax.numpy as jnp
import numpy as np
from jax import lax
from jax.experimental import pallas as pl
from jax.experimental.pallas import tpu as pltpu
from jax.sharding import PartitionSpec as P

EPSILON = 1e-06
MOMENTUM = 0.9
LEARNING_RATE = 0.001
MASKED = -1e30
MESH = pl.DeviceIdType.MESH
BF16 = jnp.bfloat16
F32 = jnp.float32
HD = 128
SCALE = HD ** (-0.5)
LOG2E = math.log2(math.e)
QB = 256
ROWS, COLS, LEN, QKV, QW = 128, 2048, 1024, 512, 256

YM, YP, X0, Y2A, Y2B, XM, XP, X2A, X2B = range(9)
HA, HB, NMA, NMB, NPA, NPB = range(6)
NX = 12


def dot(a, b):
    return jnp.dot(a, b, preferred_element_type=F32)


def dot_t(a, b):
    return lax.dot_general(a, b, (((1,), (1,)), ((), ())), preferred_element_type=F32)


def rope_tables(length):
    half = HD // 2
    inverse = np.exp(np.arange(half, dtype=np.float32) * np.float32(-2.0 * math.log(1000000.0) / HD))
    angles = np.arange(length, dtype=np.float32)[:, None] * inverse[None, :].astype(np.float32)
    cosine, sine = np.cos(angles), np.sin(angles)
    return (
        np.concatenate([cosine, cosine], axis=1).astype(np.float32),
        np.concatenate([-sine, sine], axis=1).astype(np.float32),
    )


def kernel(
    shift,
    tokens, cotangent, w_query, w_key, w_value, w_out, l_query, l_key, l_value, l_out,
    query_gain, key_gain, cosine, sine,
    o_query, o_key, o_value, o_out, o_tokens,
    tok, cot_own, normed, cots, normed_t, w_all, l_all, wo, lo, cos_t, sin_t,
    raw, q_rows, k_rows, v_rows, k_t, v_t, prob, att_t, d_att, d_keys, d_values, d_proj,
    arrived, moved, moved_out, partner, partner_out, relay,
    load_sem, store_sem, ag_send, ag_recv, rs_send, rs_recv, ex_send, ex_recv, relay_send, relay_recv,
):
    reps = lax.axis_size("rep")
    rep = lax.axis_index("rep")
    tp = lax.axis_index("tp")
    h, y = tp // 4, tp % 4
    hx, yp, ym, y2 = 1 - h, (y + 1) % 4, (y + 3) % 4, (y + 2) % 4
    ahead, behind = (rep + shift) % reps, (rep + reps - shift) % reps
    relayed = shift == 4
    ring = 16

    def along(start, by):
        return start // ring * ring + (start % ring + ring + by) % ring

    via = along(rep, -6)
    via_ahead = (along(rep, 6) + shift) % reps
    via_behind = along(behind, -6)

    def rows_of(hh, yy):
        return pl.ds(pl.multiple_of((hh * 4 + yy) * ROWS, ROWS), ROWS)

    def half_of(hh, yy, second):
        return pl.ds(pl.multiple_of((hh * 4 + yy) * ROWS + second * (ROWS // 2), ROWS // 2), ROWS // 2)

    own = rows_of(h, y)

    loads = {}

    def load(name, src, dst):
        loads[name] = pltpu.make_async_copy(src, dst, load_sem.at[len(loads)])
        loads[name].start()

    load("tok", tokens, tok)
    load("cot", cotangent, cots.at[own])
    load("cot2", cotangent, cot_own)
    load("wq", w_query, w_all.at[:, 0:256])
    load("wk", w_key, w_all.at[:, 256:384])
    load("wv", w_value, w_all.at[:, 384:512])
    load("cos", cosine, cos_t)
    load("sin", sine, sin_t)
    load("wo", w_out, wo)
    load("lo", l_out, lo)
    load("lq", l_query, l_all.at[:, 0:256])
    load("lk", l_key, l_all.at[:, 256:384])
    load("lv", l_value, l_all.at[:, 384:512])

    barrier = pltpu.get_barrier_semaphore()
    for step in range(1, 8):
        pl.semaphore_signal(barrier, inc=1, device_id={"tp": (tp + step) % 8}, device_id_type=MESH)
    partners = [ahead, behind]
    if relayed:
        partners += [via, along(rep, 6), via_ahead, via_behind]
    for device in partners:
        pl.semaphore_signal(barrier, inc=1, device_id={"rep": device}, device_id_type=MESH)

    loads["tok"].wait()
    x = tok[...].astype(F32)
    normed[own, :] = (x * lax.rsqrt(jnp.mean(x * x, axis=-1, keepdims=True) + EPSILON)).astype(BF16)
    pl.semaphore_wait(barrier, 7 + len(partners))

    t_yp, t_ym, t_x = h * 4 + yp, h * 4 + ym, hx * 4 + y
    own_half = (half_of(h, ym, 0), half_of(h, yp, 1))
    far_half = (half_of(h, y2, 0), half_of(h, y2, 1))
    plans = {
        YM: (own, t_yp),
        YP: (own, t_ym),
        X0: (own, t_x),
        Y2A: (own_half[0], t_yp),
        Y2B: (own_half[1], t_ym),
        XM: (rows_of(hx, y), t_yp),
        XP: (rows_of(hx, y), t_ym),
        X2A: (far_half[0], t_x),
        X2B: (far_half[1], t_x),
    }

    def gather(which, tag):
        rows, target = plans[tag]
        buf = (normed, cots)[which]
        return pltpu.make_async_remote_copy(
            src_ref=buf.at[rows],
            dst_ref=buf.at[rows],
            send_sem=ag_send.at[which, tag],
            recv_sem=ag_recv.at[which, tag],
            device_id={"tp": target},
            device_id_type=MESH,
        )

    def start(which, *tags):
        for tag in tags:
            gather(which, tag).start()

    def got(which, *tags):
        for tag in tags:
            gather(which, tag).wait_recv()

    def first(which):
        start(which, YM, YP, X0)

    def second(which):
        got(which, YM)
        start(which, Y2A)
        got(which, YP)
        start(which, Y2B)
        got(which, X0)
        start(which, XM, XP)

    def third(which):
        got(which, Y2A)
        start(which, X2A)
        got(which, Y2B)
        start(which, X2B)

    order = tuple(zip((0, 0, 0, 1, 0, 1, 1, 1), (0, 3, 1, 0, 2, 3, 1, 2)))

    def over_blocks(offsets, before, work, after=None):
        def body(i, carry):
            far, turn = carry
            for step, action in before.items():
                pl.when(i == step)(action)
            hh = (h + far % 2) % 2
            work(rows_of(hh, (y + turn % 4) % 4))
            for step, action in (after or {}).items():
                pl.when(i == step)(action)
            return far // 2, turn // 4

        far = sum(bit << i for i, (bit, _) in enumerate(offsets))
        turn = sum(step << (2 * i) for i, (_, step) in enumerate(offsets))
        lax.fori_loop(0, 8, body, (jnp.int32(far), jnp.int32(turn)))

    def normed_rows(values):
        return values * lax.rsqrt(jnp.mean(values * values, axis=-1, keepdims=True) + EPSILON)

    def turned(values, rows):
        return values * cos_t[rows, :] + pltpu.roll(values, HD // 2, 1) * sin_t[rows, :]

    def project(rows):
        block = normed[rows, :]
        out = dot(block, w_all[...])
        raw[rows, :] = out[:, :384]
        for head in range(2):
            q_rows[head, rows, :] = turned(
                normed_rows(out[:, head * HD : (head + 1) * HD]) * query_gain[...], rows
            ).astype(BF16)
        keys = turned(normed_rows(out[:, 256:384]) * key_gain[...], rows).astype(BF16)
        values = out[:, 384:].astype(BF16)
        k_rows[rows, :] = keys
        k_t[:, rows] = keys.T
        v_rows[rows, :] = values
        v_t[:, rows] = values.T
        normed_t[:, rows] = block.T

    def blocks_of_queries(start_at, width, work):
        def body(i, carry):
            head, at = i % 2, start_at + i // 2
            first_row = pl.multiple_of(at * QB, QB)
            work(head, first_row, pl.ds(first_row, QB), width)
            return carry

        lax.fori_loop(0, 4, body, 0)

    def forward(head, first_row, rows, width):
        scores = dot_t(k_rows[0:width, :], q_rows[head, rows, :]) * (SCALE * LOG2E)
        key_pos = lax.broadcasted_iota(jnp.int32, (width, QB), 0)
        query_pos = first_row + lax.broadcasted_iota(jnp.int32, (width, QB), 1)
        scores = jnp.where(key_pos <= query_pos, scores, MASKED)
        raised = jnp.exp2(scores - jnp.max(scores, axis=0, keepdims=True))
        p = raised * (1.0 / jnp.sum(raised, axis=0, keepdims=True))
        prob[head, 0:width, rows] = p
        out = dot(v_t[:, 0:width], p.astype(BF16))
        att_t[pl.ds(pl.multiple_of(head * HD, HD), HD), rows] = out.astype(BF16)

    def backward(head, first_row, rows, width):
        p = prob[head, 0:width, rows]
        up = d_att[head, rows, :]
        d_prob = dot_t(v_rows[0:width, :], up)
        centred = d_prob - jnp.sum(p * d_prob, axis=0, keepdims=True)
        d_scores = (p * centred * SCALE).astype(BF16)
        d_values[0:width, :] += dot(p.astype(BF16), up)
        d_keys[0:width, :] += dot(d_scores, q_rows[head, rows, :])
        d_query = dot(k_t[:, 0:width], d_scores).T
        cols = pl.ds(pl.multiple_of(head * HD, HD), HD)
        d_proj[rows, cols] = unshaped(d_query, raw[rows, cols], query_gain, rows)

    def unshaped(d_turned, before, gain, rows):
        d_grouped = d_turned * cos_t[rows, :] + pltpu.roll(d_turned * sin_t[rows, :], HD // 2, 1)
        d_norm = d_grouped * gain[...]
        inverse = lax.rsqrt(jnp.mean(before * before, axis=-1, keepdims=True) + EPSILON)
        inner = jnp.mean(before * d_norm, axis=-1, keepdims=True)
        return (inverse * d_norm - before * (inverse * inverse * inverse * inner)).astype(BF16)

    def upstream(rows):
        out = dot_t(cots[rows, :], wo[...]).astype(BF16)
        d_att[0, rows, :] = out[:, :HD]
        d_att[1, rows, :] = out[:, HD:]

    def pass_on_first():
        third(0)
        first(1)

    first(0)
    for name in ("wq", "wk", "wv", "cos", "sin", "cot"):
        loads[name].wait()
    over_blocks(
        order,
        {
            1: lambda: second(0),
            4: pass_on_first,
            5: lambda: got(0, XM, XP),
            7: lambda: got(0, X2A, X2B),
        },
        project,
    )
    second(1)
    blocks_of_queries(0, LEN // 2, forward)
    third(1)
    blocks_of_queries(2, LEN, forward)
    loads["wo"].wait()
    loads["lo"].wait()
    over_blocks(order, {5: lambda: got(1, XM, XP), 7: lambda: got(1, X2A, X2B)}, upstream)

    def exchanged(at, mine, theirs):
        return pltpu.make_async_remote_copy(
            src_ref=mine,
            dst_ref=theirs,
            send_sem=ex_send.at[at],
            recv_sem=ex_recv.at[at],
            device_id={"rep": ahead},
            device_id_type=MESH,
        )

    def exchanged_out(at):
        cols = pl.ds(pl.multiple_of(at * 512, 512), 512)
        return exchanged(at, moved_out.at[:, cols], partner_out.at[:, cols])

    def exchanged_in(at):
        rows = pl.ds(pl.multiple_of(at * 256, 256), 256)
        return exchanged(4 + at, moved.at[rows], partner.at[rows])

    def relay_first(at, mine):
        return pltpu.make_async_remote_copy(
            src_ref=mine,
            dst_ref=relay.at[at],
            send_sem=ex_send.at[4 * at + 3],
            recv_sem=relay_recv.at[at],
            device_id={"rep": via},
            device_id_type=MESH,
        )

    def relay_leg(at):
        return pltpu.make_async_remote_copy(
            src_ref=relay.at[at],
            dst_ref=partner_out.at[:, 1536:2048] if at == 0 else partner.at[1024 * at - 256 : 1024 * at],
            send_sem=relay_send.at[at],
            recv_sem=ex_recv.at[4 * at + 3],
            device_id={"rep": via_ahead},
            device_id_type=MESH,
        )

    def relay_on(at):
        if relayed:
            relay_first(at, relay.at[at]).wait_recv()
            relay_leg(at).start()

    def send_chunk(at, group, direct, mine):
        if relayed:
            pl.when(at % 4 != 3)(lambda: direct.start())
            pl.when(at % 4 == 3)(lambda: relay_first(group, mine).start())
        else:
            direct.start()

    def out_step(at, carry):
        cols = pl.ds(pl.multiple_of(at * 512, 512), 512)
        grad = dot(att_t[...], cots[:, cols])
        moved_out[:, cols] = (
            wo[:, cols].astype(F32)
            + MOMENTUM * lo[:, cols].astype(F32)
            - LEARNING_RATE * grad
        ).astype(BF16)
        send_chunk(at, 0, exchanged_out(at), moved_out.at[:, cols])
        return carry

    lax.fori_loop(0, 4, out_step, 0)
    d_keys[...] = jnp.zeros_like(d_keys)
    d_values[...] = jnp.zeros_like(d_values)
    blocks_of_queries(0, LEN // 2, backward)
    blocks_of_queries(2, LEN, backward)

    def key_step(at, carry):
        rows = pl.ds(pl.multiple_of(at * 256, 256), 256)
        d_proj[rows, 256:384] = unshaped(d_keys[rows, :], raw[rows, 256:384], key_gain, rows)
        d_proj[rows, 384:512] = d_values[rows, :].astype(BF16)
        return carry

    lax.fori_loop(0, 4, key_step, 0)

    relay_on(0)
    for which in range(2):
        for tag in plans:
            gather(which, tag).wait_send()

    terms = cots
    first_half, second_half = pl.ds(0, ROWS // 2), pl.ds(ROWS // 2, ROWS // 2)
    routes = {NX: (rows_of(hx, y), arrived.at[6], t_x)}
    for side, hh in enumerate((hx, h)):
        at, slot = 6 * side, 3 * side
        routes[at + HA] = (half_of(hh, y2, 0), arrived.at[slot, first_half], t_ym)
        routes[at + HB] = (half_of(hh, y2, 1), arrived.at[slot, second_half], t_yp)
        routes[at + NMA] = (half_of(hh, ym, 0), arrived.at[slot + 1, first_half], t_ym)
        routes[at + NMB] = (half_of(hh, ym, 1), arrived.at[slot + 1, second_half], t_ym)
        routes[at + NPA] = (half_of(hh, yp, 0), arrived.at[slot + 2, first_half], t_yp)
        routes[at + NPB] = (half_of(hh, yp, 1), arrived.at[slot + 2, second_half], t_yp)

    def scatter(tag):
        rows, dst, target = routes[tag]
        return pltpu.make_async_remote_copy(
            src_ref=terms.at[rows],
            dst_ref=dst,
            send_sem=rs_send.at[tag],
            recv_sem=rs_recv.at[tag],
            device_id={"tp": target},
            device_id_type=MESH,
        )

    def add(tag, *arrivals):
        rows = routes[tag][0]
        total = terms[rows, :].astype(F32)
        for arrival in arrivals:
            total = total + arrival.astype(F32)
        terms[rows, :] = total.astype(BF16)
        scatter(tag).start()

    def term(rows):
        terms[rows, :] = dot_t(d_proj[rows, :], w_all[...]).astype(BF16)

    def send_terms(*tags):
        def action():
            for tag in tags:
                scatter(tag).start()

        return action

    over_blocks(
        tuple((far, turn) for far in (1, 0) for turn in (2, 3, 1, 0)),
        {},
        term,
        {
            0: send_terms(HA, HB),
            1: send_terms(NMB),
            2: send_terms(NPA),
            4: send_terms(6 + HA, 6 + HB),
            5: send_terms(6 + NMB),
            6: send_terms(6 + NPA),
        },
    )

    for name in ("lq", "lk", "lv"):
        loads[name].wait()

    def weight_step(at, carry):
        rows = pl.ds(pl.multiple_of(at * 256, 256), 256)
        grad = dot(normed_t[rows, :], d_proj[...])
        moved[rows, :] = (
            w_all[rows, :].astype(F32)
            + MOMENTUM * l_all[rows, :].astype(F32)
            - LEARNING_RATE * grad
        ).astype(BF16)
        send_chunk(at, 1 + at // 4, exchanged_in(at), moved.at[rows])
        return carry

    lax.fori_loop(0, 8, weight_step, 0)

    for side in range(2):
        at, slot = 6 * side, 3 * side
        scatter(at + HA).wait_recv()
        add(at + NMA, arrived[slot, first_half, :])
        scatter(at + HB).wait_recv()
        add(at + NPB, arrived[slot, second_half, :])
    for tag in (NMA, NMB, NPA, NPB):
        scatter(tag).wait_recv()
    add(NX, arrived[1], arrived[2])
    for tag in (6 + NMA, 6 + NMB, 6 + NPA, 6 + NPB, NX):
        scatter(tag).wait_recv()
    loads["cot2"].wait()

    def token_step(at, carry):
        rows = pl.ds(pl.multiple_of(at * 32, 32), 32)
        total = terms[pl.ds(pl.multiple_of(tp * ROWS + at * 32, 32), 32), :].astype(F32)
        for slot in range(4, 7):
            total = total + arrived[slot, rows, :].astype(F32)
        x = tok[rows, :].astype(F32)
        inverse = lax.rsqrt(jnp.mean(x * x, axis=-1, keepdims=True) + EPSILON)
        inner = jnp.mean(x * total, axis=-1, keepdims=True)
        tok[rows, :] = (
            inverse * total
            - x * (inverse * inverse * inverse * inner)
            + cot_own[rows, :].astype(F32)
        ).astype(BF16)
        return carry

    lax.fori_loop(0, ROWS // 32, token_step, 0)
    store_tokens = pltpu.make_async_copy(tok, o_tokens, store_sem.at[28])
    store_tokens.start()
    relay_on(1)
    relay_on(2)

    def averaged(mine, theirs):
        return (0.5 * (mine.astype(F32) + theirs.astype(F32))).astype(BF16)

    def stored_out(at):
        cols = pl.ds(pl.multiple_of(at * 512, 512), 512)
        return (pltpu.make_async_copy(partner_out.at[:, cols], o_out.at[:, cols], store_sem.at[at]),)

    def stored_in(at):
        rows = pl.ds(pl.multiple_of(at * 256, 256), 256)
        return tuple(
            pltpu.make_async_copy(partner.at[rows, cols], out.at[rows], store_sem.at[4 + 3 * at + i])
            for i, (cols, out) in enumerate(
                ((pl.ds(0, 256), o_query), (pl.ds(256, 128), o_key), (pl.ds(384, 128), o_value))
            )
        )

    def average_out(at, carry):
        exchanged_out(at).wait_recv()
        cols = pl.ds(pl.multiple_of(at * 512, 512), 512)
        partner_out[:, cols] = averaged(moved_out[:, cols], partner_out[:, cols])
        for copy in stored_out(at):
            copy.start()
        return carry

    def average_in(at, carry):
        exchanged_in(at).wait_recv()
        rows = pl.ds(pl.multiple_of(at * 256, 256), 256)
        partner[rows, :] = averaged(moved[rows, :], partner[rows, :])
        for copy in stored_in(at):
            copy.start()
        return carry

    def finish_out(at, carry):
        exchanged_out(at).wait_send()
        for copy in stored_out(at):
            copy.wait()
        return carry

    def finish_in(at, carry):
        exchanged_in(at).wait_send()
        for copy in stored_in(at):
            copy.wait()
        return carry

    lax.fori_loop(0, 4, average_out, 0)
    lax.fori_loop(0, 8, average_in, 0)
    lax.fori_loop(0, 4, finish_out, 0)
    lax.fori_loop(0, 8, finish_in, 0)
    for tag in routes:
        scatter(tag).wait_send()
    if relayed:
        for at in range(3):
            relay_leg(at).wait_send()
    store_tokens.wait()


def training_step(exponent, arrays):
    def vmem(*shape, dtype=BF16):
        return pltpu.VMEM(shape, dtype)

    dma = pltpu.SemaphoreType.DMA
    any_spec = pl.BlockSpec(memory_space=pl.ANY)
    vmem_spec = pl.BlockSpec(memory_space=pltpu.VMEM)
    return pl.pallas_call(
        functools.partial(kernel, 1 << exponent),
        out_shape=(
            jax.ShapeDtypeStruct((COLS, 256), BF16),
            jax.ShapeDtypeStruct((COLS, 128), BF16),
            jax.ShapeDtypeStruct((COLS, 128), BF16),
            jax.ShapeDtypeStruct((256, COLS), BF16),
            jax.ShapeDtypeStruct((ROWS, COLS), BF16),
        ),
        in_specs=[any_spec] * 10 + [vmem_spec] * 2 + [any_spec] * 2,
        out_specs=(any_spec,) * 5,
        scratch_shapes=[
            vmem(ROWS, COLS),
            vmem(ROWS, COLS),
            vmem(LEN, COLS),
            vmem(LEN, COLS),
            vmem(COLS, LEN),
            vmem(COLS, QKV),
            vmem(COLS, QKV),
            vmem(QW, COLS),
            vmem(QW, COLS),
            vmem(LEN, HD, dtype=F32),
            vmem(LEN, HD, dtype=F32),
            vmem(LEN, 384, dtype=F32),
            vmem(2, LEN, HD),
            vmem(LEN, HD),
            vmem(LEN, HD),
            vmem(HD, LEN),
            vmem(HD, LEN),
            vmem(2, LEN, LEN, dtype=F32),
            vmem(QW, LEN),
            vmem(2, LEN, HD),
            vmem(LEN, HD, dtype=F32),
            vmem(LEN, HD, dtype=F32),
            vmem(LEN, QKV),
            vmem(7, ROWS, COLS),
            vmem(COLS, QKV),
            vmem(QW, COLS),
            vmem(COLS, QKV),
            vmem(QW, COLS),
            vmem(3, 256, 512),
            dma((13,)),
            dma((29,)),
            dma((2, 9)),
            dma((2, 9)),
            dma((13,)),
            dma((13,)),
            dma((12,)),
            dma((12,)),
            dma((3,)),
            dma((3,)),
        ],
        compiler_params=pltpu.CompilerParams(
            collective_id=exponent, has_side_effects=True, vmem_limit_bytes=60 << 20
        ),
        cost_estimate=pl.CostEstimate(
            flops=11_000_000_000, bytes_accessed=12_000_000, transcendentals=2_000_000
        ),
    )(*arrays)


def per_device(
    step_index, tokens, cotangent, w_query, w_key, w_value, w_out,
    last_query, last_key, last_value, last_out, query_gain, key_gain,
):
    levels = lax.axis_size("rep").bit_length() - 1
    cosine, sine = rope_tables(LEN)
    arrays = (
        tokens, cotangent, w_query[0], w_key[0], w_value[0], w_out[0],
        last_query[0], last_key[0], last_value[0], last_out[0],
        query_gain[None], key_gain[None], jnp.asarray(cosine), jnp.asarray(sine),
    )
    new_query, new_key, new_value, new_out, d_tokens = lax.switch(
        step_index[0] % levels,
        [functools.partial(training_step, exponent) for exponent in range(levels)],
        arrays,
    )
    return (new_query[None], new_key[None], new_value[None], new_out[None], d_tokens)


def solution(mesh):
    placed = (
        P(),
        P(("rep", "tp"), None),
        P(("rep", "tp"), None),
        P("rep", None, "tp"),
        P("rep", None, "tp"),
        P("rep", None, "tp"),
        P("rep", "tp", None),
        P("rep", None, "tp"),
        P("rep", None, "tp"),
        P("rep", None, "tp"),
        P("rep", "tp", None),
        P(),
        P(),
    )
    return jax.shard_map(
        per_device,
        mesh=mesh,
        in_specs=placed,
        out_specs=(
            P("rep", None, "tp"),
            P("rep", None, "tp"),
            P("rep", None, "tp"),
            P("rep", "tp", None),
            P(("rep", "tp"), None),
        ),
        check_vma=False,
    )
```
